32 devices in a mesh: sec: 8 (over z, x), op: 4 (over y, core).
Axes of the slice: x: 2, y: 2, z: 4, core: 2. Of those that a mesh axis runs over, the one named last changes fastest.
Arguments:
- state_start: bfloat16 [16, 256, 256], P('sec'), may hold values from -60 to 60
- left_ops: bfloat16 [32, 16, 256, 256], P('op', 'sec'), may hold values from -0.375 to 0.375
- right_ops: bfloat16 [32, 16, 256, 256], P('op', 'sec'), may hold values from -0.0625 to 0.0625
- shift: float32 [16], P('sec'), may hold values from 0.2 to 2.2
- partner: int32 [32, 16], P('op', 'sec'), may hold values from 0 to 5
- kept: int32 [16], P('sec'), may hold values from 128 to 256
Outputs:
- state_final: bfloat16 [16, 256, 256], P('sec')
- new_ops: bfloat16 [32, 16, 256, 256], P('op', 'sec')
The draws below stay inside these ranges and needn't reach their ends.
Inputs may be any that keep to these rules, and one draw needn't show every extreme that they name: `partner`: position in the window of 6 sector blocks.
All inputs are finite; a program needn't handle non-finite values.
Results may differ from the reference program's by a relative error of at most 0.015.
Values may be sent and summed in bfloat16 or wider, within the bound.
No kernel may reach another device: no remote copies, remote signals or barrier semaphores. Data moves between devices by JAX's collectives and lax.ppermute only.
A program may use at most 64 MiB of HBM per device.

```python
import jax
import jax.numpy as jnp
from jax import lax

M = 256
SEC_DEV = 2
ITERS = 4
SECTORS = 16
TERMS = 32


def draw_state_start(key, part):
    position = jnp.arange(SECTORS, dtype=jnp.float32) / float(SECTORS - 1)
    scale = 1.0 + 3.0 * position
    values = jnp.clip(jax.random.normal(key, (SECTORS, M, M), jnp.float32), -6.0, 6.0)
    return (values * scale[:, None, None]).astype(jnp.bfloat16)


def draw_shift(key, part):
    position = jnp.arange(SECTORS, dtype=jnp.float32) / float(SECTORS - 1)
    base = 0.3 * jnp.exp(position * jnp.log(5.0))
    factor = jnp.exp(jax.random.uniform(key, (SECTORS,), jnp.float32, -0.22, 0.22))
    return (base * factor).astype(jnp.float32)


def plant(drawn, rng, low, high):
    longest = drawn.shape.index(max(drawn.shape))
    spots = []
    for shift in (0, 1):
        where = [jax.random.randint(jax.random.fold_in(rng, axis), (), 0, length) for axis, length in enumerate(drawn.shape)]
        where[longest] = (where[longest] + shift) % drawn.shape[longest]
        spots.append(tuple(where))
    return drawn.at[spots[0]].set(low).at[spots[1]].set(high)


def steps_of(own_key, extent, cuts, least, top_value):
    factor_of = 1.0
    for dim, parts in cuts:
        steps = jax.random.uniform(jax.random.fold_in(jax.random.fold_in(own_key, 6), dim), (parts,), jnp.float32, least / len(cuts), top_value / len(cuts))
        factor_of = factor_of * jnp.repeat(jnp.exp(steps), extent[dim] // parts).reshape((-1,) + (1,) * (len(extent) - 1 - dim))
    return factor_of


def normal_values(own_key, extent, spread, bound, pieces=(), kind=jnp.bfloat16):
    gain = steps_of(own_key, extent, pieces, -0.22, 0.18) if pieces else 1.0
    values = jax.random.normal(own_key, extent, jnp.float32) * spread * gain
    return jnp.minimum(jnp.maximum(values, -bound), bound).astype(kind)


def setup_inputs(seed: int = 0) -> dict:
    seeds = jax.random.split(jax.random.key(seed), 7)
    return {
        "state_start": draw_state_start(jax.random.fold_in(seeds[6], 71), 0),
        "left_ops": normal_values(seeds[1], (TERMS, SECTORS, M, M), M ** -0.5, 0.375, ((0, 4), (1, 8))),
        "right_ops": normal_values(seeds[2], (TERMS, SECTORS, M, M), (M * TERMS) ** -0.5, 0.0625, ((0, 4), (1, 8))),
        "shift": draw_shift(jax.random.fold_in(seeds[6], 71), 0),
        "partner": plant(jax.random.randint(seeds[4], (TERMS, SECTORS), 0, 3 * SEC_DEV), jax.random.fold_in(seeds[4], 1), 0, (3 * SEC_DEV) - 1).astype(jnp.int32),
        "kept": plant(jax.random.randint(seeds[5], (SECTORS,), M // 2, M + 1), jax.random.fold_in(seeds[5], 1), M // 2, M).astype(jnp.int32),
    }


step_size = 0.5

def reference(state_start, left_ops, right_ops, shift, partner, kept):
    sector_ids = jnp.arange(SECTORS, dtype=jnp.int32)
    window_base = (sector_ids // SEC_DEV - 1) * SEC_DEV
    source = ((window_base[None, :] + partner) % SECTORS).astype(jnp.int32)
    count = float(SECTORS * M * M)

    def sigma_of(state):
        state_wide = state.astype(jnp.float32)

        def add_term(total, inputs):
            left_one, right_one, index_one = inputs
            sources = state_wide[index_one]
            halfway = jnp.einsum('bij,bjk->bik', left_one.astype(jnp.float32), sources).astype(jnp.bfloat16)
            return (total + jnp.einsum('bij,bjk->bik', halfway.astype(jnp.float32), right_one.astype(jnp.float32)), None)
        total, _ = lax.scan(add_term, jnp.zeros((SECTORS, M, M), jnp.float32), (left_ops, right_ops, source))
        return total + shift[:, None, None] * state_wide
    state = state_start
    for iteration in range(ITERS):
        sigma = sigma_of(state)
        state_wide = state.astype(jnp.float32)
        energy_sum = jnp.sum(state_wide * sigma)
        norm_sum = jnp.sum(state_wide * state_wide)
        updated = state_wide - step_size * (sigma - energy_sum / norm_sum * state_wide)
        new_norm = jnp.sum(updated * updated)
        state = (updated * jnp.sqrt(count / new_norm)).astype(jnp.bfloat16)
    columns = jnp.arange(M, dtype=jnp.int32)
    keep_mask = (columns[None, :] < kept[:, None]).astype(jnp.bfloat16)
    kept_block = state * keep_mask[:, None, :]
    kept_wide = kept_block.astype(jnp.float32)
    out_scale = 1.0 / float(M) ** 0.5

    def renorm(carry, left_one):
        projected = jnp.einsum('bij,bjk->bik', left_one.astype(jnp.float32), kept_wide).astype(jnp.bfloat16)
        result = (jnp.einsum('bji,bjk->bik', kept_wide, projected.astype(jnp.float32)) * out_scale).astype(jnp.bfloat16)
        return (carry, result)
    _, renormed = lax.scan(renorm, jnp.float32(0.0), left_ops)
    new_ops = jnp.roll(renormed, SEC_DEV, axis=1)
    return (state, new_ops)
```

```python
import functools

import jax
import jax.numpy as jnp
from jax import lax
from jax.experimental import pallas as pl
from jax.experimental.pallas import tpu as pltpu
from jax.sharding import PartitionSpec as P

ITERS = 4
step_size = 0.5
F32 = jnp.float32
BF16 = jnp.bfloat16
SMEM = pl.BlockSpec(memory_space=pltpu.SMEM)
VMEM = pl.BlockSpec(memory_space=pltpu.VMEM)


def sec_move(x, distance):
    count = lax.axis_size("sec")
    return lax.ppermute(x, "sec", [(i, (i + distance) % count) for i in range(count)])


def core_swap(x):
    return lax.ppermute(x, "op", [(i, i ^ 1) for i in range(lax.axis_size("op"))])


def chip_sum(x):
    count = lax.axis_size("op")
    chips = count // 2
    parts = [x]
    for distance in range(1, chips):
        route = [(i, (i + 2 * distance) % count) for i in range(count)]
        parts.append(lax.ppermute(x, "op", route))
    if chips == 2:
        return parts[0].astype(F32) + parts[1].astype(F32)
    me = lax.axis_index("op") // 2
    stacked = jnp.stack(parts)[(me - jnp.arange(chips)) % chips]
    total = stacked[0].astype(F32)
    for chip in range(1, chips):
        total = total + stacked[chip].astype(F32)
    return total


def apply_kernel(core, partner, *refs):
    mine, other = refs[0:3], refs[3:6]
    left, right, kept_part, sent_part, window, halfway, total = refs[6:]
    terms, sectors, width, _ = left.shape
    half = width // 2
    here = pl.ds(pl.multiple_of(core[0] * half, half), half)
    there = pl.ds(pl.multiple_of((1 - core[0]) * half, half), half)
    for group in range(3):
        for b in range(sectors):
            window[group * sectors + b, here, :] = mine[group][b]
            window[group * sectors + b, there, :] = other[group][b]
    for b in range(sectors):
        for t in range(terms):
            product = jnp.dot(left[t, b], window[partner[t, b]], preferred_element_type=F32)
            halfway[b, :, t * width : (t + 1) * width] = product.astype(BF16)
        total[b] = jnp.dot(
            halfway[b], right[:, b].reshape(terms * width, width), preferred_element_type=F32
        )
        kept_part[b] = total[b, here, :]
        sent_part[b] = total[b, there, :].astype(BF16)


def apply_terms(core, partner, mine, other, left_ops, right_ops):
    terms, sectors, width, _ = left_ops.shape
    half = (sectors, width // 2, width)
    flops = 4 * terms * sectors * width**3
    return pl.pallas_call(
        apply_kernel,
        out_shape=(
            jax.ShapeDtypeStruct(half, F32),
            jax.ShapeDtypeStruct(half, BF16),
            jax.ShapeDtypeStruct((3 * sectors, width, width), BF16),
        ),
        in_specs=[SMEM, SMEM] + [VMEM] * 8,
        out_specs=(VMEM, VMEM, VMEM),
        scratch_shapes=[
            pltpu.VMEM((sectors, width, terms * width), BF16),
            pltpu.VMEM((sectors, width, width), F32),
        ],
        compiler_params=pltpu.CompilerParams(vmem_limit_bytes=24 * 2**20),
        cost_estimate=pl.CostEstimate(flops=flops, bytes_accessed=2**22, transcendentals=0),
    )(core, partner, *mine, *other, left_ops, right_ops)


def dots_kernel(sectors, state, sigma, out):
    groups = state.shape[0] // sectors
    rows = []
    for group in range(groups):
        block = slice(group * sectors, (group + 1) * sectors)
        s = state[block].astype(F32).reshape(-1, 8, state.shape[-1])
        v = sigma[block].astype(F32).reshape(-1, 8, state.shape[-1])
        for product in (s * v, s * s, v * v):
            lanes = jnp.sum(jnp.sum(product, axis=0), axis=0, keepdims=True)
            rows.append(lanes[:, :128] + lanes[:, 128:])
    rows.append(jnp.zeros((out.shape[0] - len(rows), 128), F32))
    out[...] = jnp.concatenate(rows, axis=0)


def window_dots(state, sigma, sectors):
    return pl.pallas_call(
        functools.partial(dots_kernel, sectors),
        out_shape=jax.ShapeDtypeStruct((16, 128), F32),
        in_specs=[VMEM, VMEM],
        out_specs=VMEM,
        compiler_params=pltpu.CompilerParams(vmem_limit_bytes=16 * 2**20),
        cost_estimate=pl.CostEstimate(flops=2**22, bytes_accessed=2**21, transcendentals=0),
    )(state, sigma)


def scalars(dots, groups, first, count):
    devices = lax.axis_size("sec")
    me = lax.axis_index("sec")
    table = jnp.zeros((devices, 3, 128), F32)
    for step in range(-(-devices // groups)):
        got = dots if step == 0 else sec_move(dots, -groups * step)
        got = got[: 3 * groups].reshape(groups, 3, 128)
        for group in range(groups):
            owner = (me + step * groups + first + group) % devices
            table = lax.dynamic_update_index_in_dim(table, got[group], owner, 0)
    sums = jnp.sum(table, axis=(0, 2))
    energy_sum, norm_sum, square_sum = sums[0], sums[1], sums[2]
    a = 1.0 + step_size * (energy_sum / norm_sum)
    new_norm = a * a * norm_sum - 2.0 * step_size * a * energy_sum + step_size**2 * square_sum
    return a, jnp.sqrt(count / new_norm)


def renorm_kernel(kept_block, left, out):
    terms, sectors, width, _ = left.shape
    for b in range(sectors):
        block = kept_block[b]
        flipped = block.T
        for t in range(terms):
            projected = jnp.dot(left[t, b], block, preferred_element_type=F32).astype(BF16)
            result = jnp.dot(flipped, projected, preferred_element_type=F32)
            out[t, b] = (result * (1.0 / float(width) ** 0.5)).astype(BF16)


def renormalise(kept_block, left_ops):
    terms, sectors, width, _ = left_ops.shape
    step = 2
    blocks = pl.BlockSpec((step, sectors, width, width), lambda i: (i, 0, 0, 0))
    return pl.pallas_call(
        renorm_kernel,
        grid=(terms // step,),
        out_shape=jax.ShapeDtypeStruct(left_ops.shape, BF16),
        in_specs=[pl.BlockSpec(kept_block.shape, lambda i: (0, 0, 0)), blocks],
        out_specs=blocks,
        compiler_params=pltpu.CompilerParams(vmem_limit_bytes=24 * 2**20),
        cost_estimate=pl.CostEstimate(
            flops=4 * terms * sectors * width**3, bytes_accessed=2**22, transcendentals=0
        ),
    )(kept_block, left_ops)


def per_device(state_start, left_ops, right_ops, shift, partner, kept):
    sectors, width, _ = state_start.shape
    half = width // 2
    count = float(sectors * lax.axis_size("sec") * width * width)
    core_index = lax.axis_index("op") % 2
    core = core_index.reshape(1).astype(jnp.int32)
    shift_col = shift[:, None, None]
    moved_left = sec_move(left_ops, 1)
    moved_kept = sec_move(kept, 1)

    def halves(x):
        return (
            lax.dynamic_slice_in_dim(x, core_index * half, half, 1),
            lax.dynamic_slice_in_dim(x, (1 - core_index) * half, half, 1),
        )

    def exchange(own_half, own_other):
        before, after = sec_move(own_half, 1), sec_move(own_half, -1)
        if own_other is None:
            own_other = core_swap(own_half)
        return (before, own_half, after), (core_swap(before), own_other, core_swap(after))

    own, other = halves(state_start)
    mine, others = exchange(own, other)
    state = sigma = sigma_window = None
    for iteration in range(ITERS):
        kept_part, sent_part, window = apply_terms(core, partner, mine, others, left_ops, right_ops)
        if iteration == 0:
            state = window
        else:
            a, factor = scalars(window_dots(state, window, sectors), 3, -1, count)
            sigma_window = window
        chip_part = (kept_part + core_swap(sent_part).astype(F32)).astype(BF16)
        applied = chip_sum(chip_part) + shift_col * mine[1].astype(F32)
        if iteration == 0:
            sigma = applied
        else:
            sigma = factor * (a * sigma - step_size * applied)
            state = factor * (a * state.astype(F32) - step_size * sigma_window.astype(F32))
        rounded = sigma.astype(BF16)
        if iteration < ITERS - 1:
            mine, others = exchange(rounded, None)
    before = sec_move(rounded, 1)
    pairs = jnp.stack([before, rounded]).reshape(2 * sectors, half, width)
    swapped = core_swap(pairs)
    low = jnp.where(core_index == 0, pairs, swapped)
    high = jnp.where(core_index == 0, swapped, pairs)
    sigma_pair = jnp.concatenate([low, high], axis=1)
    state_pair = state[: 2 * sectors]
    a, factor = scalars(window_dots(state_pair, sigma_pair, sectors), 2, -1, count)
    final = (factor * (a * state_pair - step_size * sigma_pair.astype(F32))).astype(BF16)
    columns = jnp.arange(width, dtype=jnp.int32)
    keep_mask = columns[None, :] < moved_kept[:, None]
    kept_block = jnp.where(keep_mask[:, None, :], final[:sectors], jnp.zeros((), BF16))
    return final[sectors:], renormalise(kept_block, moved_left)


def solution(mesh):
    in_specs = (
        P("sec", None, None),
        P("op", "sec", None, None),
        P("op", "sec", None, None),
        P("sec"),
        P("op", "sec"),
        P("sec"),
    )
    out_specs = (P("sec", None, None), P("op", "sec", None, None))
    return jax.shard_map(
        per_device, mesh=mesh, in_specs=in_specs, out_specs=out_specs, check_vma=False
    )
```

```python
import functools

import jax
import jax.numpy as jnp
from jax import lax
from jax.experimental import pallas as pl
from jax.experimental.pallas import tpu as pltpu
from jax.sharding import PartitionSpec as P

ITERS = 4
step_size = 0.5
PLAN = (4, 4, 4, 4)
STAGE_LIMIT = 52
PACK_FLOPS = 0
GATE = False
APPLY_LIMIT = 8
F32 = jnp.float32
BF16 = jnp.bfloat16
SMEM = pl.BlockSpec(memory_space=pltpu.SMEM)
VMEM = pl.BlockSpec(memory_space=pltpu.VMEM)
ANY = pl.BlockSpec(memory_space=pl.ANY)
HBM = pl.BlockSpec(memory_space=pltpu.HBM)
MIB = 2**20


def sec_move(x, distance):
    count = lax.axis_size("sec")
    return lax.ppermute(x, "sec", [(i, (i + distance) % count) for i in range(count)])


def core_swap(x):
    return lax.ppermute(x, "op", [(i, i ^ 1) for i in range(lax.axis_size("op"))])


def chip_parts(x):
    count = lax.axis_size("op")
    chips = count // 2
    parts = [x]
    for distance in range(1, chips):
        route = [(i, (i + 2 * distance) % count) for i in range(count)]
        parts.append(lax.ppermute(x, "op", route))
    if chips <= 2:
        return parts
    me = lax.axis_index("op") // 2
    stacked = jnp.stack(parts)[(me - jnp.arange(chips)) % chips]
    return [stacked[chip] for chip in range(chips)]


def struct(shape, dtype=F32):
    return jax.ShapeDtypeStruct(shape, dtype)


def call(kernel, outs, ins, specs, limit=4, scratch=(), alias=None, flops=0):
    return pl.pallas_call(
        kernel,
        out_shape=tuple(outs),
        in_specs=specs,
        out_specs=tuple(VMEM for _ in outs),
        scratch_shapes=list(scratch),
        input_output_aliases=alias or {},
        compiler_params=pltpu.CompilerParams(vmem_limit_bytes=limit * MIB),
        cost_estimate=pl.CostEstimate(flops=flops, bytes_accessed=0, transcendentals=0),
    )(*ins)


def row_halves(core, width):
    half = width // 2
    here = pl.ds(pl.multiple_of(core[0] * half, half), half)
    there = pl.ds(pl.multiple_of((1 - core[0]) * half, half), half)
    return here, there


def first_blocks_kernel(left, out, sem):
    copy = pltpu.make_async_copy(left.at[pl.ds(0, out.shape[0])], out, sem)
    copy.start()
    copy.wait()


def first_blocks(left_ops, size):
    _, sectors, width, _ = left_ops.shape
    (terms,) = call(
        first_blocks_kernel,
        [struct((size // sectors,) + left_ops.shape[1:], BF16)],
        (left_ops,),
        [HBM],
        STAGE_LIMIT,
        [pltpu.SemaphoreType.DMA],
    )
    return terms.reshape(size, width, width)


def fill_window(rows, parts, window):
    sectors = window.shape[0] // len(parts[0])
    for side in range(2):
        for group, (ref, place) in enumerate(parts[side]):
            for b in range(sectors):
                yield group * sectors + b, rows[side], ref[place + b]


def products(partner, left, right, window, kept_part, sent_part, halfway, total, rows):
    terms, sectors, width, _ = left.shape
    for b in range(sectors):
        for t in range(terms):
            product = jnp.dot(left[t, b], window[partner[t, b]], preferred_element_type=F32)
            halfway[b, :, t * width : (t + 1) * width] = product.astype(BF16)
        total[b] = jnp.dot(
            halfway[b], right[:, b].reshape(terms * width, width), preferred_element_type=F32
        )
        kept_part[b] = total[b, rows[0], :]
        sent_part[b] = total[b, rows[1], :].astype(BF16)


def emit_blocks(left, first, outs):
    sectors = left.shape[1]
    for out in outs:
        for i in range(out.shape[0]):
            out[i] = left[(first + i) // sectors, (first + i) % sectors]
        first += out.shape[0]


def window_pieces(sectors, own, own_other, pair, pair_other):
    mine = [(pair, 0), (own, 0), (pair, sectors)]
    other = [(pair_other, 0), (own_other, 0), (pair_other, sectors)]
    return mine, other


def first_apply_kernel(emit, core, partner, left, right, *refs):
    pieces, (kept_part, sent_part, window, *blocks, halfway, total) = refs[:4], refs[4:]
    rows = row_halves(core, left.shape[-1])
    for place, row, value in fill_window(rows, window_pieces(left.shape[1], *pieces), window):
        window[place, row, :] = value
    emit_blocks(left, emit, blocks)
    products(partner, left, right, window, kept_part, sent_part, halfway, total, rows)


def step_factors(count, sums):
    sums = jnp.sum(sums, axis=1, keepdims=True)
    energy_sum, norm_sum, square_sum = sums[0:1], sums[1:2], sums[2:3]
    a = 1.0 + step_size * (energy_sum / norm_sum)
    new_norm = a * a * norm_sum - 2.0 * step_size * a * energy_sum + step_size**2 * square_sum
    factor = jnp.sqrt(count / new_norm)
    return factor * a, -step_size * factor


def apply_kernel(emit, count, core, partner, left, right, *refs):
    pieces, refs = refs[:4], refs[4:]
    sums, state, kept_part, sent_part, window, *blocks, halfway, total = refs
    rows = row_halves(core, left.shape[-1])
    alpha, beta = step_factors(count, sums[...])
    for place, row, value in fill_window(rows, window_pieces(left.shape[1], *pieces), window):
        new = alpha * state[place, row, :].astype(F32) + beta * value.astype(F32)
        window[place, row, :] = new.astype(BF16)
    emit_blocks(left, emit, blocks)
    products(partner, left, right, window, kept_part, sent_part, halfway, total, rows)


def apply_terms(core, partner, pieces, left, right, count, sums, state, emit, sizes):
    terms, sectors, width, _ = left.shape
    half = (sectors, width // 2, width)
    outs = [struct(half), struct(half, BF16), struct((3 * sectors, width, width), BF16)]
    outs += [struct((size, width, width), BF16) for size in sizes]
    scratch = [
        pltpu.VMEM((sectors, width, terms * width), BF16),
        pltpu.VMEM((sectors, width, width), F32),
    ]
    ins = (core, partner, left, right, *pieces)
    specs = [SMEM, SMEM] + [VMEM] * 6
    if sums is None:
        kernel = functools.partial(first_apply_kernel, emit)
        return call(kernel, outs, ins, specs, APPLY_LIMIT, scratch)
    kernel = functools.partial(apply_kernel, emit, count)
    specs += [VMEM, VMEM]
    return call(kernel, outs, ins + (sums, state), specs, APPLY_LIMIT, scratch, {9: 2})


def combine_kernel(count, core, shift, state, *refs):
    parts, (rounded, sums) = refs[:count], refs[-2:]
    sectors, half, width = rounded.shape
    here, _ = row_halves(core, width)
    totals = [jnp.zeros((8, width), F32) for _ in range(3)]
    for b in range(sectors):
        total = parts[0][b].astype(F32)
        for part in parts[1:]:
            total = total + part[b].astype(F32)
        s = state[sectors + b, here, :].astype(F32)
        total = total + shift[b] * s
        rounded[b] = total.astype(BF16)
        for i, product in enumerate((s * total, s * s, total * total)):
            totals[i] = totals[i] + jnp.sum(product.reshape(-1, 8, width), axis=0)
    lines = []
    for total in totals:
        lanes = jnp.sum(total, axis=0, keepdims=True)
        lines.append(sum(lanes[:, i : i + 128] for i in range(0, width, 128)))
    lines.append(jnp.zeros((5, 128), F32))
    sums[...] = jnp.concatenate(lines, axis=0)


def pack_kernel(before, after, *refs):
    out = refs[-1]
    sectors = before.shape[0]
    out[:sectors] = before[...]
    out[sectors:] = after[...]


def hold_kernel(*refs):
    pass


def hold(x, *after):
    specs = [VMEM] + [ANY] * len(after)
    return call(hold_kernel, [struct(x.shape, x.dtype)], (x, *after), specs, alias={0: 0})[0]


def finish_kernel(count, sizes, core, kept, sums, state, own, own_other, before, before_other, *refs):
    pieces, refs = refs[: len(sizes)], refs[len(sizes) :]
    final, new_ops, window, results, sems = refs
    sectors, width, _ = final.shape
    alpha, beta = step_factors(count, sums[...])
    rows = row_halves(core, width)
    parts = ([(before, 0), (own, 0)], [(before_other, 0), (own_other, 0)])
    for place, row, value in fill_window(rows, parts, window):
        new = alpha * state[place, row, :].astype(F32) + beta * value.astype(F32)
        window[place, row, :] = new.astype(BF16)
    final[...] = window[sectors:]
    columns = lax.broadcasted_iota(jnp.int32, (width, width), 1)
    blocks = []
    for b in range(sectors):
        block = jnp.where(columns < kept[b], window[b].astype(F32), 0.0).astype(BF16)
        blocks.append((block, block.T))
    copies = []
    unit = 0
    for piece, size in zip(pieces, sizes):
        for i in range(size):
            t, b = unit // sectors, unit % sectors
            block, flipped = blocks[b]
            projected = jnp.dot(piece[i], block, preferred_element_type=F32).astype(BF16)
            result = jnp.dot(flipped, projected, preferred_element_type=F32)
            results[t, b] = (result * (1.0 / float(width) ** 0.5)).astype(BF16)
            if b == sectors - 1:
                copy = pltpu.make_async_copy(results.at[t], new_ops.at[t], sems.at[t])
                copy.start()
                copies.append(copy)
            unit += 1
    for copy in copies:
        copy.wait()


def xor_sum(x, axes, masks):
    size = 1
    for axis in axes:
        size *= lax.axis_size(axis)

    def other(mask):
        return lax.ppermute(x, axes, [(i, i ^ mask) for i in range(size)])

    if len(masks) == 1:
        return x + other(masks[0])
    low, high = masks
    both, one, two = other(low ^ high), other(low), other(high)
    return (x + one) + (two + both)


def far_sums(sums):
    devices = lax.axis_size("sec")
    bits = [1 << i for i in range(1, devices.bit_length() - 1)][::-1]
    while bits:
        sums = xor_sum(sums, ("sec",), bits[:2])
        bits = bits[2:]
    return sums


def near_sums(sums):
    return xor_sum(sums, ("sec", "op"), [1, lax.axis_size("op")])


def per_device(state_start, left_ops, right_ops, shift, partner, kept):
    terms, sectors, width, _ = left_ops.shape
    half = width // 2
    devices = lax.axis_size("sec")
    count = float(sectors * devices * width * width)
    core_index = lax.axis_index("op") % 2
    core = core_index.reshape(1).astype(jnp.int32)
    half_shape = (sectors, half, width)
    units = terms * sectors
    plan = list(PLAN[:-1]) + [units - sum(PLAN[:-1])]

    def pack(before, after):
        (pair,) = call(
            pack_kernel,
            [struct((2 * sectors, half, width), BF16)],
            (before, after),
            [VMEM, VMEM],
            flops=PACK_FLOPS,
        )
        return pair

    own = lax.dynamic_slice_in_dim(state_start, core_index * half, half, 1)
    own_other = lax.dynamic_slice_in_dim(state_start, (1 - core_index) * half, half, 1)
    pair = pack(sec_move(own, 1), sec_move(own, -1))
    pieces = [sec_move(first_blocks(left_ops, plan[0]), 1)]
    moved_kept = sec_move(kept, 1)
    sums = state = None
    for iteration in range(ITERS):
        kept_part, sent_part, state, *blocks = apply_terms(
            core,
            partner,
            (own, own_other, pair, core_swap(pair)),
            left_ops,
            right_ops,
            count,
            sums,
            state,
            sum(plan[: iteration + 1]),
            plan[iteration + 1 : iteration + 2],
        )
        chip_part = (kept_part + core_swap(sent_part).astype(F32)).astype(BF16)
        parts = chip_parts(chip_part)
        gates = [pieces[-1]] + ([moved_kept] if iteration == 0 else [])
        own, sums = call(
            functools.partial(combine_kernel, len(parts)),
            [struct(half_shape, BF16), struct((8, 128))],
            (core, shift, state, *parts, *gates),
            [SMEM, SMEM] + [VMEM] * (1 + len(parts)) + [ANY] * len(gates),
        )
        sums = far_sums(sums)
        own_other = core_swap(own)
        before = sec_move(own, 1)
        if iteration < ITERS - 1:
            pair = pack(before, sec_move(own, -1))
            if GATE:
                pair = hold(pair, sums)
            sums = near_sums(sums)
            pieces.append(sec_move(blocks[0], 1))
    if GATE:
        before = hold(before, sums)
    sums = near_sums(sums)
    final, new_ops = pl.pallas_call(
        functools.partial(finish_kernel, count, tuple(plan)),
        out_shape=(struct(state_start.shape, BF16), struct(left_ops.shape, BF16)),
        in_specs=[SMEM] * 2 + [VMEM] * (6 + len(pieces)),
        out_specs=(VMEM, ANY),
        scratch_shapes=[
            pltpu.VMEM((2 * sectors, width, width), BF16),
            pltpu.VMEM(left_ops.shape, BF16),
            pltpu.SemaphoreType.DMA((terms,)),
        ],
        compiler_params=pltpu.CompilerParams(vmem_limit_bytes=8 * MIB),
        cost_estimate=pl.CostEstimate(
            flops=4 * terms * sectors * width**3, bytes_accessed=4 * MIB, transcendentals=0
        ),
    )(core, moved_kept, sums, state, own, own_other, before, core_swap(before), *pieces)
    return final, new_ops


def solution(mesh):
    in_specs = (
        P("sec", None, None),
        P("op", "sec", None, None),
        P("op", "sec", None, None),
        P("sec"),
        P("op", "sec"),
        P("sec"),
    )
    out_specs = (P("sec", None, None), P("op", "sec", None, None))
    return jax.shard_map(
        per_device, mesh=mesh, in_specs=in_specs, out_specs=out_specs, check_vma=False
    )
```

```python
import functools

import jax
import jax.numpy as jnp
from jax import lax
from jax.experimental import pallas as pl
from jax.experimental.pallas import tpu as pltpu
from jax.sharding import PartitionSpec as P

ITERS = 4
step_size = 0.5
PLAN = (4, 5, 5, 2)
THREE = True
LATE = (1, 2, 3)
STAGE_LIMIT = 52
APPLY_LIMIT = 8
F32 = jnp.float32
BF16 = jnp.bfloat16
SMEM = pl.BlockSpec(memory_space=pltpu.SMEM)
VMEM = pl.BlockSpec(memory_space=pltpu.VMEM)
ANY = pl.BlockSpec(memory_space=pl.ANY)
HBM = pl.BlockSpec(memory_space=pltpu.HBM)
MIB = 2**20


def sec_move(x, distance):
    count = lax.axis_size("sec")
    return lax.ppermute(x, "sec", [(i, (i + distance) % count) for i in range(count)])


def core_swap(x):
    return lax.ppermute(x, "op", [(i, i ^ 1) for i in range(lax.axis_size("op"))])


def chip_parts(x):
    count = lax.axis_size("op")
    chips = count // 2
    parts = [x]
    for distance in range(1, chips):
        route = [(i, (i + 2 * distance) % count) for i in range(count)]
        parts.append(lax.ppermute(x, "op", route))
    if chips <= 2:
        return parts
    me = lax.axis_index("op") // 2
    stacked = jnp.stack(parts)[(me - jnp.arange(chips)) % chips]
    return [stacked[chip] for chip in range(chips)]


def struct(shape, dtype=F32):
    return jax.ShapeDtypeStruct(shape, dtype)


def call(kernel, outs, ins, specs, limit=4, scratch=(), alias=None):
    return pl.pallas_call(
        kernel,
        out_shape=tuple(outs),
        in_specs=specs,
        out_specs=tuple(VMEM for _ in outs),
        scratch_shapes=list(scratch),
        input_output_aliases=alias or {},
        compiler_params=pltpu.CompilerParams(vmem_limit_bytes=limit * MIB),
        cost_estimate=pl.CostEstimate(flops=0, bytes_accessed=0, transcendentals=0),
    )(*ins)


def row_halves(core, width):
    half = width // 2
    here = pl.ds(pl.multiple_of(core[0] * half, half), half)
    there = pl.ds(pl.multiple_of((1 - core[0]) * half, half), half)
    return here, there


def first_blocks_kernel(left, out, sems):
    sectors = left.shape[1]
    copies = [
        pltpu.make_async_copy(left.at[i // sectors, i % sectors], out.at[i], sems.at[i])
        for i in range(out.shape[0])
    ]
    for copy in copies:
        copy.start()
    for copy in copies:
        copy.wait()


def first_blocks(left_ops, size):
    width = left_ops.shape[-1]
    return call(
        first_blocks_kernel,
        [struct((size, width, width), BF16)],
        (left_ops,),
        [HBM],
        STAGE_LIMIT,
        [pltpu.SemaphoreType.DMA((size,))],
    )[0]


def fill_window(rows, parts, window):
    sectors = window.shape[0] // len(parts[0])
    for side in range(2):
        for group, (ref, place) in enumerate(parts[side]):
            for b in range(sectors):
                yield group * sectors + b, rows[side], ref[place + b]


def products(partner, left, right, window, kept_part, sent_part, halfway, total, rows):
    terms, sectors, width, _ = left.shape
    for b in range(sectors):
        for t in range(terms):
            product = jnp.dot(left[t, b], window[partner[t, b]], preferred_element_type=F32)
            halfway[b, :, t * width : (t + 1) * width] = product.astype(BF16)
        total[b] = jnp.dot(
            halfway[b], right[:, b].reshape(terms * width, width), preferred_element_type=F32
        )
        kept_part[b] = total[b, rows[0], :]
        sent_part[b] = total[b, rows[1], :].astype(BF16)


def emit_blocks(left, first, outs):
    sectors = left.shape[1]
    for out in outs:
        for i in range(out.shape[0]):
            out[i] = left[(first + i) // sectors, (first + i) % sectors]
        first += out.shape[0]


def window_pieces(sectors, own, own_other, pair, pair_other):
    mine = [(pair, 0), (own, 0), (pair, sectors)]
    other = [(pair_other, 0), (own_other, 0), (pair_other, sectors)]
    return mine, other


def first_apply_kernel(emit, core, partner, left, right, *refs):
    pieces, (kept_part, sent_part, window, *blocks, halfway, total) = refs[:4], refs[4:]
    rows = row_halves(core, left.shape[-1])
    for place, row, value in fill_window(rows, window_pieces(left.shape[1], *pieces), window):
        window[place, row, :] = value
    emit_blocks(left, emit, blocks)
    products(partner, left, right, window, kept_part, sent_part, halfway, total, rows)


def step_factors(count, sums):
    sums = jnp.sum(sums, axis=1, keepdims=True)
    energy_sum, norm_sum, square_sum = sums[0:1], sums[1:2], sums[2:3]
    a = 1.0 + step_size * (energy_sum / norm_sum)
    new_norm = a * a * norm_sum - 2.0 * step_size * a * energy_sum + step_size**2 * square_sum
    factor = jnp.sqrt(count / new_norm)
    return factor * a, -step_size * factor


def apply_kernel(emit, count, core, partner, left, right, *refs):
    pieces, refs = refs[:4], refs[4:]
    sums, state, kept_part, sent_part, window, *blocks, halfway, total = refs
    rows = row_halves(core, left.shape[-1])
    alpha, beta = step_factors(count, sums[...])
    for place, row, value in fill_window(rows, window_pieces(left.shape[1], *pieces), window):
        new = alpha * state[place, row, :].astype(F32) + beta * value.astype(F32)
        window[place, row, :] = new.astype(BF16)
    emit_blocks(left, emit, blocks)
    products(partner, left, right, window, kept_part, sent_part, halfway, total, rows)


def apply_terms(core, partner, pieces, left, right, count, sums, state, emit, sizes):
    terms, sectors, width, _ = left.shape
    half = (sectors, width // 2, width)
    outs = [struct(half), struct(half, BF16), struct((3 * sectors, width, width), BF16)]
    outs += [struct((size, width, width), BF16) for size in sizes]
    scratch = [
        pltpu.VMEM((sectors, width, terms * width), BF16),
        pltpu.VMEM((sectors, width, width), F32),
    ]
    ins = (core, partner, left, right, *pieces)
    specs = [SMEM, SMEM] + [VMEM] * 6
    if sums is None:
        kernel = functools.partial(first_apply_kernel, emit)
        return call(kernel, outs, ins, specs, APPLY_LIMIT, scratch)
    kernel = functools.partial(apply_kernel, emit, count)
    specs += [VMEM, VMEM]
    return call(kernel, outs, ins + (sums, state), specs, APPLY_LIMIT, scratch, {9: 2})


def combine_kernel(count, core, shift, state, *refs):
    parts, (rounded, sums) = refs[:count], refs[-2:]
    sectors, half, width = rounded.shape
    here, _ = row_halves(core, width)
    totals = [jnp.zeros((8, width), F32) for _ in range(3)]
    for b in range(sectors):
        total = parts[0][b].astype(F32)
        for part in parts[1:]:
            total = total + part[b].astype(F32)
        s = state[sectors + b, here, :].astype(F32)
        total = total + shift[b] * s
        rounded[b] = total.astype(BF16)
        for i, product in enumerate((s * total, s * s, total * total)):
            totals[i] = totals[i] + jnp.sum(product.reshape(-1, 8, width), axis=0)
    lines = []
    for total in totals:
        lanes = jnp.sum(total, axis=0, keepdims=True)
        lines.append(sum(lanes[:, i : i + 128] for i in range(0, width, 128)))
    lines.append(jnp.zeros((5, 128), F32))
    sums[...] = jnp.concatenate(lines, axis=0)


def pack_kernel(*refs):
    *parts, out = refs
    held = parts[0].shape[0]
    for i, part in enumerate(parts):
        out[i * held : (i + 1) * held] = part[...]


def hold_kernel(*refs):
    pass


def hold(x, *after):
    specs = [VMEM] + [ANY] * len(after)
    return call(hold_kernel, [struct(x.shape, x.dtype)], (x, *after), specs, alias={0: 0})[0]


def finish_kernel(count, sizes, core, kept, sums, state, pair, pair_other, *refs):
    pieces, refs = refs[: len(sizes)], refs[len(sizes) :]
    final, new_ops, window, results, sems = refs
    sectors, width, _ = final.shape
    alpha, beta = step_factors(count, sums[...])
    rows = row_halves(core, width)
    parts = [[(ref, 0), (ref, sectors)] for ref in (pair, pair_other)]
    for place, row, value in fill_window(rows, parts, window):
        new = alpha * state[place, row, :].astype(F32) + beta * value.astype(F32)
        window[place, row, :] = new.astype(BF16)
    final[...] = window[sectors:]
    columns = lax.broadcasted_iota(jnp.int32, (width, width), 1)
    blocks = []
    for b in range(sectors):
        block = jnp.where(columns < kept[b], window[b].astype(F32), 0.0).astype(BF16)
        blocks.append((block, block.T))
    copies = []
    unit = 0
    for piece, size in zip(pieces, sizes):
        for i in range(size):
            t, b = unit // sectors, unit % sectors
            block, flipped = blocks[b]
            projected = jnp.dot(piece[i], block, preferred_element_type=F32).astype(BF16)
            result = jnp.dot(flipped, projected, preferred_element_type=F32)
            results[t, b] = (result * (1.0 / float(width) ** 0.5)).astype(BF16)
            if b == sectors - 1:
                copy = pltpu.make_async_copy(results.at[t], new_ops.at[t], sems.at[t])
                copy.start()
                copies.append(copy)
            unit += 1
    for copy in copies:
        copy.wait()


def xor_sum(x, axes, masks, late=()):
    size = 1
    for axis in axes:
        size *= lax.axis_size(axis)

    def other(mask, sent):
        return lax.ppermute(sent, axes, [(i, i ^ mask) for i in range(size)])

    last = hold(x, *late) if late else x

    if len(masks) == 1:
        return x + other(masks[0], last)
    low, high = masks
    both, one, two = other(low ^ high, x), other(low, x), other(high, last)
    return (x + one) + (two + both)


def far_sums(sums, late):
    devices = lax.axis_size("sec")
    bits = [1 << i for i in range(1, devices.bit_length() - 1)][::-1]
    while bits:
        sums = xor_sum(sums, ("sec",), bits[:2], late)
        bits, late = bits[2:], ()
    return sums


def near_sums(sums):
    return xor_sum(sums, ("sec", "op"), [1, lax.axis_size("op")])


def per_device(state_start, left_ops, right_ops, shift, partner, kept):
    terms, sectors, width, _ = left_ops.shape
    half = width // 2
    devices = lax.axis_size("sec")
    count = float(sectors * devices * width * width)
    core_index = lax.axis_index("op") % 2
    core = core_index.reshape(1).astype(jnp.int32)
    half_shape = (sectors, half, width)
    units = terms * sectors
    plan = list(PLAN[:-1]) + [units - sum(PLAN[:-1])]
    plan = [size for size in plan if size]

    def pack(*parts):
        return call(
            pack_kernel,
            [struct((2 * sectors, half, width), BF16)],
            parts,
            [VMEM] * len(parts),
        )[0]

    own = lax.dynamic_slice_in_dim(state_start, core_index * half, half, 1)
    own_other = lax.dynamic_slice_in_dim(state_start, (1 - core_index) * half, half, 1)
    before, after = sec_move(own, 1), sec_move(own, -1)
    first = first_blocks(left_ops, plan[0])
    pair = pack(before, hold(after, first))
    pieces = [sec_move(first, 1)]
    moved_kept = sec_move(kept, 1)
    sums = state = None
    for iteration in range(ITERS):
        kept_part, sent_part, state, *blocks = apply_terms(
            core,
            partner,
            (own, own_other, pair, core_swap(pair)),
            left_ops,
            right_ops,
            count,
            sums,
            state,
            sum(plan[: iteration + 1]),
            plan[iteration + 1 : iteration + 2],
        )
        chip_part = (kept_part + core_swap(sent_part).astype(F32)).astype(BF16)
        parts = chip_parts(chip_part)
        gates = [moved_kept] if iteration == 0 else []
        late = [pieces[-1]] if len(pieces) > iteration else []
        if iteration not in LATE:
            gates, late = gates + late, []
        own, sums = call(
            functools.partial(combine_kernel, len(parts)),
            [struct(half_shape, BF16), struct((8, 128))],
            (core, shift, state, *parts, *gates),
            [SMEM, SMEM] + [VMEM] * (1 + len(parts)) + [ANY] * len(gates),
        )
        sums = far_sums(sums, late)
        if iteration < ITERS - 1:
            own_other = core_swap(own)
            pair = pack(sec_move(own, 1), sec_move(own, -1))
            if blocks:
                pieces.append(sec_move(blocks[0], 1))
        else:
            pair = pack(sec_move(own, 1), own)
        sums = near_sums(sums)
    pair_other = core_swap(pair)
    final, new_ops = pl.pallas_call(
        functools.partial(finish_kernel, count, tuple(plan)),
        out_shape=(struct(state_start.shape, BF16), struct(left_ops.shape, BF16)),
        in_specs=[SMEM] * 2 + [VMEM] * (4 + len(pieces)),
        out_specs=(VMEM, ANY),
        scratch_shapes=[
            pltpu.VMEM((2 * sectors, width, width), BF16),
            pltpu.VMEM(left_ops.shape, BF16),
            pltpu.SemaphoreType.DMA((terms,)),
        ],
        compiler_params=pltpu.CompilerParams(vmem_limit_bytes=8 * MIB),
        cost_estimate=pl.CostEstimate(
            flops=4 * terms * sectors * width**3, bytes_accessed=4 * MIB, transcendentals=0
        ),
    )(core, moved_kept, sums, state, pair, pair_other, *pieces)
    return final, new_ops


def solution(mesh):
    in_specs = (
        P("sec", None, None),
        P("op", "sec", None, None),
        P("op", "sec", None, None),
        P("sec"),
        P("op", "sec"),
        P("sec"),
    )
    out_specs = (P("sec", None, None), P("op", "sec", None, None))
    return jax.shard_map(
        per_device, mesh=mesh, in_specs=in_specs, out_specs=out_specs, check_vma=False
    )
```

```python
import functools

import jax
import jax.numpy as jnp
from jax import lax
from jax.experimental import pallas as pl
from jax.experimental.pallas import tpu as pltpu
from jax.sharding import PartitionSpec as P

ITERS = 4
step_size = 0.5
PLAN = (4, 5, 5, 2)
THREE = True
LATE = (1, 2, 3)
STAGE_LIMIT = 52
APPLY_LIMIT = 8
F32 = jnp.float32
BF16 = jnp.bfloat16
SMEM = pl.BlockSpec(memory_space=pltpu.SMEM)
VMEM = pl.BlockSpec(memory_space=pltpu.VMEM)
ANY = pl.BlockSpec(memory_space=pl.ANY)
HBM = pl.BlockSpec(memory_space=pltpu.HBM)
MIB = 2**20


def sec_move(x, distance):
    count = lax.axis_size("sec")
    return lax.ppermute(x, "sec", [(i, (i + distance) % count) for i in range(count)])


def core_swap(x):
    return lax.ppermute(x, "op", [(i, i ^ 1) for i in range(lax.axis_size("op"))])


def chip_parts(x):
    count = lax.axis_size("op")
    chips = count // 2
    parts = [x]
    for distance in range(1, chips):
        route = [(i, (i + 2 * distance) % count) for i in range(count)]
        parts.append(lax.ppermute(x, "op", route))
    if chips <= 2:
        return parts
    me = lax.axis_index("op") // 2
    stacked = jnp.stack(parts)[(me - jnp.arange(chips)) % chips]
    return [stacked[chip] for chip in range(chips)]


def struct(shape, dtype=F32):
    return jax.ShapeDtypeStruct(shape, dtype)


def call(kernel, outs, ins, specs, limit=4, scratch=(), alias=None):
    return pl.pallas_call(
        kernel,
        out_shape=tuple(outs),
        in_specs=specs,
        out_specs=tuple(VMEM for _ in outs),
        scratch_shapes=list(scratch),
        input_output_aliases=alias or {},
        compiler_params=pltpu.CompilerParams(vmem_limit_bytes=limit * MIB),
        cost_estimate=pl.CostEstimate(flops=0, bytes_accessed=0, transcendentals=0),
    )(*ins)


def row_halves(width):
    half = width // 2
    core = lax.rem(lax.axis_index("op"), 2)
    here = pl.ds(pl.multiple_of(core * half, half), half)
    there = pl.ds(pl.multiple_of((1 - core) * half, half), half)
    return here, there


def first_blocks_kernel(left, out, sems):
    sectors = left.shape[1]
    copies = [
        pltpu.make_async_copy(left.at[i // sectors, i % sectors], out.at[i], sems.at[i])
        for i in range(out.shape[0])
    ]
    for copy in copies:
        copy.start()
    for copy in copies:
        copy.wait()


def first_blocks(left_ops, size):
    width = left_ops.shape[-1]
    return call(
        first_blocks_kernel,
        [struct((size, width, width), BF16)],
        (left_ops,),
        [HBM],
        STAGE_LIMIT,
        [pltpu.SemaphoreType.DMA((size,))],
    )[0]


def fill_window(rows, parts, window):
    sectors = window.shape[0] // len(parts[0])
    for side in range(2):
        for group, (ref, place) in enumerate(parts[side]):
            for b in range(sectors):
                yield group * sectors + b, rows[side], ref[place + b]


def products(partner_in, partner, left, right, window, kept_part, sent_part, halfway, total, rows):
    terms, sectors, width, _ = left.shape
    partner_in.wait()
    for b in range(sectors):
        for t in range(terms):
            product = jnp.dot(left[t, b], window[partner[t, b]], preferred_element_type=F32)
            halfway[b, :, t * width : (t + 1) * width] = product.astype(BF16)
        total[b] = jnp.dot(
            halfway[b], right[:, b].reshape(terms * width, width), preferred_element_type=F32
        )
        kept_part[b] = total[b, rows[0], :]
        sent_part[b] = total[b, rows[1], :].astype(BF16)


def emit_blocks(left, first, outs):
    sectors = left.shape[1]
    for out in outs:
        for i in range(out.shape[0]):
            out[i] = left[(first + i) // sectors, (first + i) % sectors]
        first += out.shape[0]


def window_pieces(sectors, own, own_other, pair, pair_other):
    mine = [(pair, 0), (own, 0), (pair, sectors)]
    other = [(pair_other, 0), (own_other, 0), (pair_other, sectors)]
    return mine, other


def first_apply_kernel(emit, partner_any, left, right, *refs):
    pieces, refs = refs[:4], refs[4:]
    kept_part, sent_part, window, *blocks, halfway, total, partner, sem = refs
    partner_in = pltpu.make_async_copy(partner_any, partner, sem)
    partner_in.start()
    rows = row_halves(left.shape[-1])
    for place, row, value in fill_window(rows, window_pieces(left.shape[1], *pieces), window):
        window[place, row, :] = value
    emit_blocks(left, emit, blocks)
    products(partner_in, partner, left, right, window, kept_part, sent_part, halfway, total, rows)


def step_factors(count, sums):
    sums = jnp.sum(sums, axis=1, keepdims=True)
    energy_sum, norm_sum, square_sum = sums[0:1], sums[1:2], sums[2:3]
    a = 1.0 + step_size * (energy_sum / norm_sum)
    new_norm = a * a * norm_sum - 2.0 * step_size * a * energy_sum + step_size**2 * square_sum
    factor = jnp.sqrt(count / new_norm)
    return factor * a, -step_size * factor


def apply_kernel(emit, count, partner_any, left, right, *refs):
    pieces, refs = refs[:4], refs[4:]
    sums, state, kept_part, sent_part, window, *blocks, halfway, total, partner, sem = refs
    partner_in = pltpu.make_async_copy(partner_any, partner, sem)
    partner_in.start()
    rows = row_halves(left.shape[-1])
    alpha, beta = step_factors(count, sums[...])
    for place, row, value in fill_window(rows, window_pieces(left.shape[1], *pieces), window):
        new = alpha * state[place, row, :].astype(F32) + beta * value.astype(F32)
        window[place, row, :] = new.astype(BF16)
    emit_blocks(left, emit, blocks)
    products(partner_in, partner, left, right, window, kept_part, sent_part, halfway, total, rows)


def apply_terms(partner, pieces, left, right, count, sums, state, emit, sizes):
    terms, sectors, width, _ = left.shape
    half = (sectors, width // 2, width)
    outs = [struct(half), struct(half, BF16), struct((3 * sectors, width, width), BF16)]
    outs += [struct((size, width, width), BF16) for size in sizes]
    scratch = [
        pltpu.VMEM((sectors, width, terms * width), BF16),
        pltpu.VMEM((sectors, width, width), F32),
        pltpu.SMEM(partner.shape, partner.dtype),
        pltpu.SemaphoreType.DMA,
    ]
    ins = (partner, left, right, *pieces)
    specs = [ANY] + [VMEM] * 6
    if sums is None:
        kernel = functools.partial(first_apply_kernel, emit)
        return call(kernel, outs, ins, specs, APPLY_LIMIT, scratch)
    kernel = functools.partial(apply_kernel, emit, count)
    specs += [VMEM, VMEM]
    return call(kernel, outs, ins + (sums, state), specs, APPLY_LIMIT, scratch, {8: 2})


def combine_kernel(count, shift, state, *refs):
    parts, (rounded, sums) = refs[:count], refs[-2:]
    sectors, half, width = rounded.shape
    here, _ = row_halves(width)
    totals = [jnp.zeros((8, width), F32) for _ in range(3)]
    for b in range(sectors):
        total = parts[0][b].astype(F32)
        for part in parts[1:]:
            total = total + part[b].astype(F32)
        s = state[sectors + b, here, :].astype(F32)
        total = total + shift[b : b + 1, 0:1] * s
        rounded[b] = total.astype(BF16)
        for i, product in enumerate((s * total, s * s, total * total)):
            totals[i] = totals[i] + jnp.sum(product.reshape(-1, 8, width), axis=0)
    lines = []
    for total in totals:
        lanes = jnp.sum(total, axis=0, keepdims=True)
        lines.append(sum(lanes[:, i : i + 128] for i in range(0, width, 128)))
    lines.append(jnp.zeros((5, 128), F32))
    sums[...] = jnp.concatenate(lines, axis=0)


def pack_kernel(*refs):
    *parts, out = refs
    held = parts[0].shape[0]
    for i, part in enumerate(parts):
        out[i * held : (i + 1) * held] = part[...]


def hold_kernel(*refs):
    pass


def hold(x, *after):
    specs = [VMEM] + [ANY] * len(after)
    return call(hold_kernel, [struct(x.shape, x.dtype)], (x, *after), specs, alias={0: 0})[0]


def finish_kernel(count, sizes, kept, sums, state, pair, pair_other, *refs):
    pieces, refs = refs[: len(sizes)], refs[len(sizes) :]
    final, new_ops, window, projected, results, sems, final_sem = refs
    sectors, width, _ = final.shape
    alpha, beta = step_factors(count, sums[...])
    rows = row_halves(width)
    units = [(piece, i) for piece, size in zip(pieces, sizes) for i in range(size)]
    columns = lax.broadcasted_iota(jnp.int32, (width, width), 1)
    scale = 1.0 / float(width) ** 0.5
    flipped = []

    def fill(group):
        for ref, row in zip((pair, pair_other), rows):
            for b in range(sectors):
                place = group * sectors + b
                value = beta * ref[place].astype(F32)
                new = alpha * state[place, row, :].astype(F32) + value
                window[place, row, :] = new.astype(BF16)

    fill(0)
    fill(1)
    final_out = pltpu.make_async_copy(window.at[pl.ds(sectors, sectors)], final, final_sem)
    final_out.start()
    for b in range(sectors):
        block = jnp.where(columns < kept[b : b + 1, 0:1], window[b].astype(F32), 0.0)
        flipped.append((block * scale).astype(BF16).T)
        block = block.astype(BF16)
        for t, (piece, i) in enumerate(units[b::sectors]):
            product = jnp.dot(piece[i], block, preferred_element_type=F32)
            projected[b, :, t * width : (t + 1) * width] = product.astype(BF16)
    copies = []
    for b in range(sectors):
        for t in range(len(units) // sectors):
            part = projected[b, :, t * width : (t + 1) * width]
            result = jnp.dot(flipped[b], part, preferred_element_type=F32)
            results[t, b] = result.astype(BF16)
            copy = pltpu.make_async_copy(
                results.at[t, b], new_ops.at[t, b], sems.at[t * sectors + b]
            )
            copy.start()
            copies.append(copy)
    final_out.wait()
    for copy in copies:
        copy.wait()


def xor_sum(x, axes, masks, late=()):
    size = 1
    for axis in axes:
        size *= lax.axis_size(axis)

    def other(mask, sent):
        return lax.ppermute(sent, axes, [(i, i ^ mask) for i in range(size)])

    last = hold(x, *late) if late else x

    if len(masks) == 1:
        return x + other(masks[0], last)
    low, high = masks
    both, one, two = other(low ^ high, x), other(low, x), other(high, last)
    return (x + one) + (two + both)


def far_sums(sums, late):
    devices = lax.axis_size("sec")
    bits = [1 << i for i in range(1, devices.bit_length() - 1)][::-1]
    while bits:
        sums = xor_sum(sums, ("sec",), bits[:2], late)
        bits, late = bits[2:], ()
    return sums


def near_sums(sums):
    return xor_sum(sums, ("sec", "op"), [1, lax.axis_size("op")])


def per_device(state_start, left_ops, right_ops, shift, partner, kept):
    terms, sectors, width, _ = left_ops.shape
    half = width // 2
    devices = lax.axis_size("sec")
    count = float(sectors * devices * width * width)
    core_index = lax.axis_index("op") % 2
    shifts = jnp.broadcast_to(shift[:, None], (sectors, 128))
    kepts = jnp.broadcast_to(kept[:, None], (sectors, 128))
    half_shape = (sectors, half, width)
    units = terms * sectors
    plan = list(PLAN[:-1]) + [units - sum(PLAN[:-1])]
    plan = [size for size in plan if size]

    def pack(*parts):
        return call(
            pack_kernel,
            [struct((2 * sectors, half, width), BF16)],
            parts,
            [VMEM] * len(parts),
        )[0]

    own = lax.dynamic_slice_in_dim(state_start, core_index * half, half, 1)
    own_other = lax.dynamic_slice_in_dim(state_start, (1 - core_index) * half, half, 1)
    before, after = sec_move(own, 1), sec_move(own, -1)
    first = first_blocks(left_ops, plan[0])
    pair = pack(before, hold(after, first))
    pieces = [sec_move(first, 1)]
    moved_kept = sec_move(kepts, 1)
    sums = state = None
    for iteration in range(ITERS):
        kept_part, sent_part, state, *blocks = apply_terms(
            partner,
            (own, own_other, pair, core_swap(pair)),
            left_ops,
            right_ops,
            count,
            sums,
            state,
            sum(plan[: iteration + 1]),
            plan[iteration + 1 : iteration + 2],
        )
        chip_part = (kept_part + core_swap(sent_part).astype(F32)).astype(BF16)
        parts = chip_parts(chip_part)
        gates = [moved_kept] if iteration == 0 else []
        late = [pieces[-1]] if len(pieces) > iteration else []
        if iteration not in LATE:
            gates, late = gates + late, []
        own, sums = call(
            functools.partial(combine_kernel, len(parts)),
            [struct(half_shape, BF16), struct((8, 128))],
            (shifts, state, *parts, *gates),
            [VMEM] * (2 + len(parts)) + [ANY] * len(gates),
        )
        sums = far_sums(sums, late)
        if iteration < ITERS - 1:
            own_other = core_swap(own)
            pair = pack(sec_move(own, 1), sec_move(own, -1))
            if blocks:
                pieces.append(sec_move(blocks[0], 1))
        else:
            pair = pack(sec_move(own, 1), own)
        sums = near_sums(sums)
    pair_other = core_swap(pair)
    final, new_ops = pl.pallas_call(
        functools.partial(finish_kernel, count, tuple(plan)),
        out_shape=(struct(state_start.shape, BF16), struct(left_ops.shape, BF16)),
        in_specs=[VMEM] * (5 + len(pieces)),
        out_specs=(ANY, ANY),
        scratch_shapes=[
            pltpu.VMEM((2 * sectors, width, width), BF16),
            pltpu.VMEM((sectors, width, terms * width), BF16),
            pltpu.VMEM(left_ops.shape, BF16),
            pltpu.SemaphoreType.DMA((units,)),
            pltpu.SemaphoreType.DMA,
        ],
        compiler_params=pltpu.CompilerParams(vmem_limit_bytes=8 * MIB),
        cost_estimate=pl.CostEstimate(
            flops=4 * terms * sectors * width**3, bytes_accessed=4 * MIB, transcendentals=0
        ),
    )(moved_kept, sums, state, pair, pair_other, *pieces)
    return final, new_ops


def solution(mesh):
    in_specs = (
        P("sec", None, None),
        P("op", "sec", None, None),
        P("op", "sec", None, None),
        P("sec"),
        P("op", "sec"),
        P("sec"),
    )
    out_specs = (P("sec", None, None), P("op", "sec", None, None))
    return jax.shard_map(
        per_device, mesh=mesh, in_specs=in_specs, out_specs=out_specs, check_vma=False
    )
```

```python
import functools

import jax
import jax.numpy as jnp
from jax import lax
from jax.experimental import pallas as pl
from jax.experimental.pallas import tpu as pltpu
from jax.sharding import PartitionSpec as P

ITERS = 4
step_size = 0.5
PLAN = (4, 5, 5, 2)
THREE = True
LATE = (1, 2, 3)
STAGE_LIMIT = 52
APPLY_LIMIT = 8
F32 = jnp.float32
BF16 = jnp.bfloat16
SMEM = pl.BlockSpec(memory_space=pltpu.SMEM)
VMEM = pl.BlockSpec(memory_space=pltpu.VMEM)
ANY = pl.BlockSpec(memory_space=pl.ANY)
HBM = pl.BlockSpec(memory_space=pltpu.HBM)
MIB = 2**20


def sec_move(x, distance):
    count = lax.axis_size("sec")
    return lax.ppermute(x, "sec", [(i, (i + distance) % count) for i in range(count)])


def core_swap(x):
    return lax.ppermute(x, "op", [(i, i ^ 1) for i in range(lax.axis_size("op"))])


def chip_parts(x):
    count = lax.axis_size("op")
    chips = count // 2
    parts = [x]
    for distance in range(1, chips):
        route = [(i, (i + 2 * distance) % count) for i in range(count)]
        parts.append(lax.ppermute(x, "op", route))
    if chips <= 2:
        return parts
    me = lax.axis_index("op") // 2
    stacked = jnp.stack(parts)[(me - jnp.arange(chips)) % chips]
    return [stacked[chip] for chip in range(chips)]


def struct(shape, dtype=F32):
    return jax.ShapeDtypeStruct(shape, dtype)


def call(kernel, outs, ins, specs, limit=4, scratch=(), alias=None):
    return pl.pallas_call(
        kernel,
        out_shape=tuple(outs),
        in_specs=specs,
        out_specs=tuple(VMEM for _ in outs),
        scratch_shapes=list(scratch),
        input_output_aliases=alias or {},
        compiler_params=pltpu.CompilerParams(vmem_limit_bytes=limit * MIB),
        cost_estimate=pl.CostEstimate(flops=0, bytes_accessed=0, transcendentals=0),
    )(*ins)


def row_halves(width):
    half = width // 2
    core = lax.rem(lax.axis_index("op"), 2)
    here = pl.ds(pl.multiple_of(core * half, half), half)
    there = pl.ds(pl.multiple_of((1 - core) * half, half), half)
    return here, there


def first_blocks_kernel(left, out, sems):
    sectors = left.shape[1]
    copies = [
        pltpu.make_async_copy(left.at[i // sectors, i % sectors], out.at[i], sems.at[i])
        for i in range(out.shape[0])
    ]
    for copy in copies:
        copy.start()
    for copy in copies:
        copy.wait()


def first_blocks(left_ops, size):
    width = left_ops.shape[-1]
    return call(
        first_blocks_kernel,
        [struct((size, width, width), BF16)],
        (left_ops,),
        [HBM],
        STAGE_LIMIT,
        [pltpu.SemaphoreType.DMA((size,))],
    )[0]


def fill_window(rows, parts, window):
    sectors = window.shape[0] // len(parts[0])
    for side in range(2):
        for group, (ref, place) in enumerate(parts[side]):
            for b in range(sectors):
                yield group * sectors + b, rows[side], ref[place + b]


def products(partner_in, partner, left, right, window, kept_part, sent_part, halfway, total, rows):
    terms, sectors, width, _ = left.shape
    partner_in.wait()
    for b in range(sectors):
        for t in range(terms):
            product = jnp.dot(left[t, b], window[partner[t, b]], preferred_element_type=F32)
            halfway[b, :, t * width : (t + 1) * width] = product.astype(BF16)
        total[b] = jnp.dot(
            halfway[b], right[:, b].reshape(terms * width, width), preferred_element_type=F32
        )
        kept_part[b] = total[b, rows[0], :]
        sent_part[b] = total[b, rows[1], :].astype(BF16)


def emit_blocks(left, first, outs):
    sectors = left.shape[1]
    for out in outs:
        for i in range(out.shape[0]):
            out[i] = left[(first + i) // sectors, (first + i) % sectors]
        first += out.shape[0]


def window_pieces(sectors, own, own_other, pair, pair_other):
    mine = [(pair, 0), (own, 0), (pair, sectors)]
    other = [(pair_other, 0), (own_other, 0), (pair_other, sectors)]
    return mine, other


def first_apply_kernel(emit, partner_any, left, right, *refs):
    pieces, refs = refs[:4], refs[4:]
    kept_part, sent_part, window, *blocks, halfway, total, partner, sem = refs
    partner_in = pltpu.make_async_copy(partner_any, partner, sem)
    partner_in.start()
    rows = row_halves(left.shape[-1])
    for place, row, value in fill_window(rows, window_pieces(left.shape[1], *pieces), window):
        window[place, row, :] = value
    emit_blocks(left, emit, blocks)
    products(partner_in, partner, left, right, window, kept_part, sent_part, halfway, total, rows)


def step_factors(count, sums):
    sums = jnp.sum(sums, axis=1, keepdims=True)
    energy_sum, norm_sum, square_sum = sums[0:1], sums[1:2], sums[2:3]
    a = 1.0 + step_size * (energy_sum / norm_sum)
    new_norm = a * a * norm_sum - 2.0 * step_size * a * energy_sum + step_size**2 * square_sum
    factor = jnp.sqrt(count / new_norm)
    return factor * a, -step_size * factor


def apply_kernel(emit, count, partner_any, left, right, *refs):
    pieces, refs = refs[:4], refs[4:]
    sums, state, kept_part, sent_part, window, *blocks, halfway, total, partner, sem = refs
    partner_in = pltpu.make_async_copy(partner_any, partner, sem)
    partner_in.start()
    rows = row_halves(left.shape[-1])
    alpha, beta = step_factors(count, sums[...])
    for place, row, value in fill_window(rows, window_pieces(left.shape[1], *pieces), window):
        new = alpha * state[place, row, :].astype(F32) + beta * value.astype(F32)
        window[place, row, :] = new.astype(BF16)
    emit_blocks(left, emit, blocks)
    products(partner_in, partner, left, right, window, kept_part, sent_part, halfway, total, rows)


def apply_terms(partner, pieces, left, right, count, sums, state, emit, sizes):
    terms, sectors, width, _ = left.shape
    half = (sectors, width // 2, width)
    outs = [struct(half), struct(half, BF16), struct((3 * sectors, width, width), BF16)]
    outs += [struct((size, width, width), BF16) for size in sizes]
    scratch = [
        pltpu.VMEM((sectors, width, terms * width), BF16),
        pltpu.VMEM((sectors, width, width), F32),
        pltpu.SMEM(partner.shape, partner.dtype),
        pltpu.SemaphoreType.DMA,
    ]
    ins = (partner, left, right, *pieces)
    specs = [ANY] + [VMEM] * 6
    if sums is None:
        kernel = functools.partial(first_apply_kernel, emit)
        return call(kernel, outs, ins, specs, APPLY_LIMIT, scratch)
    kernel = functools.partial(apply_kernel, emit, count)
    specs += [VMEM, VMEM]
    return call(kernel, outs, ins + (sums, state), specs, APPLY_LIMIT, scratch, {8: 2})


def combine_kernel(count, shift, state, *refs):
    parts, (rounded, sums) = refs[:count], refs[-2:]
    sectors, half, width = rounded.shape
    here, _ = row_halves(width)
    totals = [jnp.zeros((8, width), F32) for _ in range(3)]
    for b in range(sectors):
        total = parts[0][b].astype(F32)
        for part in parts[1:]:
            total = total + part[b].astype(F32)
        s = state[sectors + b, here, :].astype(F32)
        total = total + shift[b : b + 1, 0:1] * s
        rounded[b] = total.astype(BF16)
        for i, product in enumerate((s * total, s * s, total * total)):
            totals[i] = totals[i] + jnp.sum(product.reshape(-1, 8, width), axis=0)
    lines = []
    for total in totals:
        lanes = jnp.sum(total, axis=0, keepdims=True)
        lines.append(sum(lanes[:, i : i + 128] for i in range(0, width, 128)))
    lines.append(jnp.zeros((5, 128), F32))
    sums[...] = jnp.concatenate(lines, axis=0)


def pack_kernel(*refs):
    *parts, out = refs
    held = parts[0].shape[0]
    for i, part in enumerate(parts):
        out[i * held : (i + 1) * held] = part[...]


def hold_kernel(*refs):
    pass


def hold(x, *after):
    specs = [VMEM] + [ANY] * len(after)
    return call(hold_kernel, [struct(x.shape, x.dtype)], (x, *after), specs, alias={0: 0})[0]


def finish_kernel(count, sizes, kept, sums, state, pair, pair_other, *refs):
    pieces, refs = refs[: len(sizes)], refs[len(sizes) :]
    final, new_ops, window, projected, results, sems, final_sem = refs
    sectors, width, _ = final.shape
    alpha, beta = step_factors(count, sums[...])
    rows = row_halves(width)
    units = [(piece, i) for piece, size in zip(pieces, sizes) for i in range(size)]
    columns = lax.broadcasted_iota(jnp.int32, (width, width), 1)
    scale = 1.0 / float(width) ** 0.5

    def fill(group):
        for ref, row in zip((pair, pair_other), rows):
            for b in range(sectors):
                place = group * sectors + b
                value = beta * ref[place].astype(F32)
                new = alpha * state[place, row, :].astype(F32) + value
                window[place, row, :] = new.astype(BF16)

    fill(0)
    copies = []
    for b in range(sectors):
        block = jnp.where(columns < kept[b : b + 1, 0:1], window[b].astype(F32), 0.0)
        flipped = (block * scale).astype(BF16).T
        block = block.astype(BF16)
        for t, (piece, i) in enumerate(units[b::sectors]):
            product = jnp.dot(piece[i], block, preferred_element_type=F32)
            projected[b, :, t * width : (t + 1) * width] = product.astype(BF16)
        for t in range(len(units) // sectors):
            part = projected[b, :, t * width : (t + 1) * width]
            result = jnp.dot(flipped, part, preferred_element_type=F32)
            results[t, b] = result.astype(BF16)
            copy = pltpu.make_async_copy(
                results.at[t, b], new_ops.at[t, b], sems.at[t * sectors + b]
            )
            copy.start()
            copies.append(copy)
        if b == 0:
            fill(1)
            final_out = pltpu.make_async_copy(
                window.at[pl.ds(sectors, sectors)], final, final_sem
            )
            final_out.start()
    final_out.wait()
    for copy in copies:
        copy.wait()


def xor_sum(x, axes, masks, late=()):
    size = 1
    for axis in axes:
        size *= lax.axis_size(axis)

    def other(mask, sent):
        return lax.ppermute(sent, axes, [(i, i ^ mask) for i in range(size)])

    last = hold(x, *late) if late else x

    if len(masks) == 1:
        return x + other(masks[0], last)
    low, high = masks
    both, one, two = other(low ^ high, x), other(low, x), other(high, last)
    return (x + one) + (two + both)


def far_sums(sums, late):
    devices = lax.axis_size("sec")
    bits = [1 << i for i in range(1, devices.bit_length() - 1)][::-1]
    while bits:
        sums = xor_sum(sums, ("sec",), bits[:2], late)
        bits, late = bits[2:], ()
    return sums


def near_sums(sums):
    return xor_sum(sums, ("sec", "op"), [1, lax.axis_size("op")])


def per_device(state_start, left_ops, right_ops, shift, partner, kept):
    terms, sectors, width, _ = left_ops.shape
    half = width // 2
    devices = lax.axis_size("sec")
    count = float(sectors * devices * width * width)
    core_index = lax.axis_index("op") % 2
    shifts = jnp.broadcast_to(shift[:, None], (sectors, 128))
    kepts = jnp.broadcast_to(kept[:, None], (sectors, 128))
    half_shape = (sectors, half, width)
    units = terms * sectors
    plan = list(PLAN[:-1]) + [units - sum(PLAN[:-1])]
    plan = [size for size in plan if size]

    def pack(*parts):
        return call(
            pack_kernel,
            [struct((2 * sectors, half, width), BF16)],
            parts,
            [VMEM] * len(parts),
        )[0]

    own = lax.dynamic_slice_in_dim(state_start, core_index * half, half, 1)
    own_other = lax.dynamic_slice_in_dim(state_start, (1 - core_index) * half, half, 1)
    before, after = sec_move(own, 1), sec_move(own, -1)
    first = first_blocks(left_ops, plan[0])
    pair = pack(before, hold(after, first))
    pieces = [sec_move(first, 1)]
    moved_kept = sec_move(kepts, 1)
    sums = state = None
    for iteration in range(ITERS):
        kept_part, sent_part, state, *blocks = apply_terms(
            partner,
            (own, own_other, pair, core_swap(pair)),
            left_ops,
            right_ops,
            count,
            sums,
            state,
            sum(plan[: iteration + 1]),
            plan[iteration + 1 : iteration + 2],
        )
        chip_part = (kept_part + core_swap(sent_part).astype(F32)).astype(BF16)
        parts = chip_parts(chip_part)
        gates = [moved_kept] if iteration == 0 else []
        late = [pieces[-1]] if len(pieces) > iteration else []
        if iteration not in LATE:
            gates, late = gates + late, []
        own, sums = call(
            functools.partial(combine_kernel, len(parts)),
            [struct(half_shape, BF16), struct((8, 128))],
            (shifts, state, *parts, *gates),
            [VMEM] * (2 + len(parts)) + [ANY] * len(gates),
        )
        sums = far_sums(sums, late)
        if iteration < ITERS - 1:
            own_other = core_swap(own)
            pair = pack(sec_move(own, 1), sec_move(own, -1))
            if blocks:
                pieces.append(sec_move(blocks[0], 1))
        else:
            pair = pack(sec_move(own, 1), own)
        sums = near_sums(sums)
    pair_other = core_swap(pair)
    final, new_ops = pl.pallas_call(
        functools.partial(finish_kernel, count, tuple(plan)),
        out_shape=(struct(state_start.shape, BF16), struct(left_ops.shape, BF16)),
        in_specs=[VMEM] * (5 + len(pieces)),
        out_specs=(ANY, ANY),
        scratch_shapes=[
            pltpu.VMEM((2 * sectors, width, width), BF16),
            pltpu.VMEM((sectors, width, terms * width), BF16),
            pltpu.VMEM(left_ops.shape, BF16),
            pltpu.SemaphoreType.DMA((units,)),
            pltpu.SemaphoreType.DMA,
        ],
        compiler_params=pltpu.CompilerParams(vmem_limit_bytes=8 * MIB),
        cost_estimate=pl.CostEstimate(
            flops=4 * terms * sectors * width**3, bytes_accessed=4 * MIB, transcendentals=0
        ),
    )(moved_kept, sums, state, pair, pair_other, *pieces)
    return final, new_ops


def solution(mesh):
    in_specs = (
        P("sec", None, None),
        P("op", "sec", None, None),
        P("op", "sec", None, None),
        P("sec"),
        P("op", "sec"),
        P("sec"),
    )
    out_specs = (P("sec", None, None), P("op", "sec", None, None))
    return jax.shard_map(
        per_device, mesh=mesh, in_specs=in_specs, out_specs=out_specs, check_vma=False
    )
```

```python
import functools

import jax
import jax.numpy as jnp
from jax import lax
from jax.experimental import pallas as pl
from jax.experimental.pallas import tpu as pltpu
from jax.sharding import PartitionSpec as P

ITERS = 4
step_size = 0.5
PLAN = (4, 5, 5, 2)
THREE = True
LATE = (1, 2, 3)
STAGE_LIMIT = 52
APPLY_LIMIT = 8
F32 = jnp.float32
BF16 = jnp.bfloat16
SMEM = pl.BlockSpec(memory_space=pltpu.SMEM)
VMEM = pl.BlockSpec(memory_space=pltpu.VMEM)
ANY = pl.BlockSpec(memory_space=pl.ANY)
HBM = pl.BlockSpec(memory_space=pltpu.HBM)
MIB = 2**20


def sec_move(x, distance):
    count = lax.axis_size("sec")
    return lax.ppermute(x, "sec", [(i, (i + distance) % count) for i in range(count)])


def core_swap(x):
    return lax.ppermute(x, "op", [(i, i ^ 1) for i in range(lax.axis_size("op"))])


def chip_parts(x):
    count = lax.axis_size("op")
    chips = count // 2
    parts = [x]
    for distance in range(1, chips):
        route = [(i, (i + 2 * distance) % count) for i in range(count)]
        parts.append(lax.ppermute(x, "op", route))
    if chips <= 2:
        return parts
    me = lax.axis_index("op") // 2
    stacked = jnp.stack(parts)[(me - jnp.arange(chips)) % chips]
    return [stacked[chip] for chip in range(chips)]


def struct(shape, dtype=F32):
    return jax.ShapeDtypeStruct(shape, dtype)


def call(kernel, outs, ins, specs, limit=4, scratch=(), alias=None):
    return pl.pallas_call(
        kernel,
        out_shape=tuple(outs),
        in_specs=specs,
        out_specs=tuple(VMEM for _ in outs),
        scratch_shapes=list(scratch),
        input_output_aliases=alias or {},
        compiler_params=pltpu.CompilerParams(vmem_limit_bytes=limit * MIB),
        cost_estimate=pl.CostEstimate(flops=0, bytes_accessed=0, transcendentals=0),
    )(*ins)


def row_halves(width):
    half = width // 2
    core = lax.rem(lax.axis_index("op"), 2)
    here = pl.ds(pl.multiple_of(core * half, half), half)
    there = pl.ds(pl.multiple_of((1 - core) * half, half), half)
    return here, there


def first_blocks_kernel(left, out, sems):
    sectors = left.shape[1]
    copies = [
        pltpu.make_async_copy(left.at[i // sectors, i % sectors], out.at[i], sems.at[i])
        for i in range(out.shape[0])
    ]
    for copy in copies:
        copy.start()
    for copy in copies:
        copy.wait()


def first_blocks(left_ops, size):
    width = left_ops.shape[-1]
    return call(
        first_blocks_kernel,
        [struct((size, width, width), BF16)],
        (left_ops,),
        [HBM],
        STAGE_LIMIT,
        [pltpu.SemaphoreType.DMA((size,))],
    )[0]


def fill_window(rows, parts, window):
    sectors = window.shape[0] // len(parts[0])
    for side in range(2):
        for group, (ref, place) in enumerate(parts[side]):
            for b in range(sectors):
                yield group * sectors + b, rows[side], ref[place + b]


def products(partner_in, partner, left, right, window, kept_part, sent_part, halfway, total, rows):
    terms, sectors, width, _ = left.shape
    partner_in.wait()
    for b in range(sectors):
        for t in range(terms):
            product = jnp.dot(left[t, b], window[partner[t, b]], preferred_element_type=F32)
            halfway[b, :, t * width : (t + 1) * width] = product.astype(BF16)
        total[b] = jnp.dot(
            halfway[b], right[:, b].reshape(terms * width, width), preferred_element_type=F32
        )
        kept_part[b] = total[b, rows[0], :]
        sent_part[b] = total[b, rows[1], :].astype(BF16)


def emit_blocks(left, first, outs):
    sectors = left.shape[1]
    for out in outs:
        for i in range(out.shape[0]):
            out[i] = left[(first + i) // sectors, (first + i) % sectors]
        first += out.shape[0]


def window_pieces(sectors, own, own_other, pair, pair_other):
    mine = [(pair, 0), (own, 0), (pair, sectors)]
    other = [(pair_other, 0), (own_other, 0), (pair_other, sectors)]
    return mine, other


def first_apply_kernel(emit, partner_any, left, right, *refs):
    pieces, refs = refs[:4], refs[4:]
    kept_part, sent_part, window, *blocks, halfway, total, partner, sem = refs
    partner_in = pltpu.make_async_copy(partner_any, partner, sem)
    partner_in.start()
    rows = row_halves(left.shape[-1])
    for place, row, value in fill_window(rows, window_pieces(left.shape[1], *pieces), window):
        window[place, row, :] = value
    emit_blocks(left, emit, blocks)
    products(partner_in, partner, left, right, window, kept_part, sent_part, halfway, total, rows)


def step_factors(count, sums):
    sums = jnp.sum(sums, axis=1, keepdims=True)
    energy_sum, norm_sum, square_sum = sums[0:1], sums[1:2], sums[2:3]
    a = 1.0 + step_size * (energy_sum / norm_sum)
    new_norm = a * a * norm_sum - 2.0 * step_size * a * energy_sum + step_size**2 * square_sum
    factor = jnp.sqrt(count / new_norm)
    return factor * a, -step_size * factor


def apply_kernel(emit, count, partner_any, left, right, *refs):
    pieces, refs = refs[:4], refs[4:]
    sums, state, kept_part, sent_part, window, *blocks, halfway, total, partner, sem = refs
    partner_in = pltpu.make_async_copy(partner_any, partner, sem)
    partner_in.start()
    rows = row_halves(left.shape[-1])
    alpha, beta = step_factors(count, sums[...])
    for place, row, value in fill_window(rows, window_pieces(left.shape[1], *pieces), window):
        new = alpha * state[place, row, :].astype(F32) + beta * value.astype(F32)
        window[place, row, :] = new.astype(BF16)
    emit_blocks(left, emit, blocks)
    products(partner_in, partner, left, right, window, kept_part, sent_part, halfway, total, rows)


def apply_terms(partner, pieces, left, right, count, sums, state, emit, sizes):
    terms, sectors, width, _ = left.shape
    half = (sectors, width // 2, width)
    outs = [struct(half), struct(half, BF16), struct((3 * sectors, width, width), BF16)]
    outs += [struct((size, width, width), BF16) for size in sizes]
    scratch = [
        pltpu.VMEM((sectors, width, terms * width), BF16),
        pltpu.VMEM((sectors, width, width), F32),
        pltpu.SMEM(partner.shape, partner.dtype),
        pltpu.SemaphoreType.DMA,
    ]
    ins = (partner, left, right, *pieces)
    specs = [ANY] + [VMEM] * 6
    if sums is None:
        kernel = functools.partial(first_apply_kernel, emit)
        return call(kernel, outs, ins, specs, APPLY_LIMIT, scratch)
    kernel = functools.partial(apply_kernel, emit, count)
    specs += [VMEM, VMEM]
    return call(kernel, outs, ins + (sums, state), specs, APPLY_LIMIT, scratch, {8: 2})


def combine_kernel(count, shift, state, *refs):
    parts, (rounded, sums) = refs[:count], refs[-2:]
    sectors, half, width = rounded.shape
    here, _ = row_halves(width)
    totals = [jnp.zeros((8, width), F32) for _ in range(3)]
    for b in range(sectors):
        total = parts[0][b].astype(F32)
        for part in parts[1:]:
            total = total + part[b].astype(F32)
        s = state[sectors + b, here, :].astype(F32)
        total = total + shift[b : b + 1, 0:1] * s
        rounded[b] = total.astype(BF16)
        for i, product in enumerate((s * total, s * s, total * total)):
            totals[i] = totals[i] + jnp.sum(product.reshape(-1, 8, width), axis=0)
    lines = []
    for total in totals:
        lanes = jnp.sum(total, axis=0, keepdims=True)
        lines.append(sum(lanes[:, i : i + 128] for i in range(0, width, 128)))
    lines.append(jnp.zeros((5, 128), F32))
    sums[...] = jnp.concatenate(lines, axis=0)


def pack_kernel(*refs):
    *parts, out = refs
    held = parts[0].shape[0]
    for i, part in enumerate(parts):
        out[i * held : (i + 1) * held] = part[...]


def hold_kernel(*refs):
    pass


def hold(x, *after):
    specs = [VMEM] + [ANY] * len(after)
    return call(hold_kernel, [struct(x.shape, x.dtype)], (x, *after), specs, alias={0: 0})[0]


def finish_kernel(count, sizes, kept, sums, state, pair, pair_other, *refs):
    pieces, refs = refs[: len(sizes)], refs[len(sizes) :]
    final, new_ops, window, projected, results, sems, final_sem = refs
    sectors, width, _ = final.shape
    alpha, beta = step_factors(count, sums[...])
    rows = row_halves(width)
    units = [(piece, i) for piece, size in zip(pieces, sizes) for i in range(size)]
    columns = lax.broadcasted_iota(jnp.int32, (width, width), 1)
    scale = 1.0 / float(width) ** 0.5

    def fill(group):
        for ref, row in zip((pair, pair_other), rows):
            for b in range(sectors):
                place = group * sectors + b
                value = beta * ref[place].astype(F32)
                new = alpha * state[place, row, :].astype(F32) + value
                window[place, row, :] = new.astype(BF16)

    fill(0)
    copies = []
    for b in range(sectors):
        block = jnp.where(columns < kept[b : b + 1, 0:1], window[b].astype(F32), 0.0)
        flipped = (block * scale).astype(BF16).T
        block = block.astype(BF16)
        for t, (piece, i) in enumerate(units[b::sectors]):
            product = jnp.dot(piece[i], block, preferred_element_type=F32)
            projected[b, :, t * width : (t + 1) * width] = product.astype(BF16)
        for t in range(len(units) // sectors):
            part = projected[b, :, t * width : (t + 1) * width]
            result = jnp.dot(flipped, part, preferred_element_type=F32)
            results[t, b] = result.astype(BF16)
            copy = pltpu.make_async_copy(
                results.at[t, b], new_ops.at[t, b], sems.at[t * sectors + b]
            )
            copy.start()
            copies.append(copy)
        if b == 0:
            fill(1)
            final_out = pltpu.make_async_copy(
                window.at[pl.ds(sectors, sectors)], final, final_sem
            )
            final_out.start()
    final_out.wait()
    for copy in copies:
        copy.wait()


def xor_sum(x, axes, masks, late=()):
    size = 1
    for axis in axes:
        size *= lax.axis_size(axis)

    def other(mask, sent):
        return lax.ppermute(sent, axes, [(i, i ^ mask) for i in range(size)])

    last = hold(x, *late) if late else x

    if len(masks) == 1:
        return x + other(masks[0], last)
    low, high = masks
    both, one, two = other(low ^ high, x), other(low, x), other(high, last)
    return (x + one) + (two + both)


def far_sums(sums, late):
    devices = lax.axis_size("sec")
    bits = [1 << i for i in range(1, devices.bit_length() - 1)][::-1]
    while bits:
        sums = xor_sum(sums, ("sec",), bits[:2], late)
        bits, late = bits[2:], ()
    return sums


def near_sums(sums):
    return xor_sum(sums, ("sec", "op"), [1, lax.axis_size("op")])


def per_device(state_start, left_ops, right_ops, shift, partner, kept):
    terms, sectors, width, _ = left_ops.shape
    half = width // 2
    devices = lax.axis_size("sec")
    count = float(sectors * devices * width * width)
    core_index = lax.axis_index("op") % 2
    shifts = jnp.broadcast_to(shift[:, None], (sectors, 128))
    kepts = jnp.broadcast_to(kept[:, None], (sectors, 128))
    half_shape = (sectors, half, width)
    units = terms * sectors
    plan = list(PLAN[:-1]) + [units - sum(PLAN[:-1])]
    plan = [size for size in plan if size]

    def pack(*parts):
        return call(
            pack_kernel,
            [struct((2 * sectors, half, width), BF16)],
            parts,
            [VMEM] * len(parts),
        )[0]

    own = lax.dynamic_slice_in_dim(state_start, core_index * half, half, 1)
    own_other = lax.dynamic_slice_in_dim(state_start, (1 - core_index) * half, half, 1)
    before, after = sec_move(own, 1), sec_move(own, -1)
    first = first_blocks(left_ops, plan[0])
    pair = pack(before, hold(after, first))
    pieces = [sec_move(first, 1)]
    moved_kept = sec_move(kepts, 1)
    sums = state = None
    for iteration in range(ITERS):
        kept_part, sent_part, state, *blocks = apply_terms(
            partner,
            (own, own_other, pair, core_swap(pair)),
            left_ops,
            right_ops,
            count,
            sums,
            state,
            sum(plan[: iteration + 1]),
            plan[iteration + 1 : iteration + 2],
        )
        chip_part = (kept_part + core_swap(sent_part).astype(F32)).astype(BF16)
        parts = chip_parts(chip_part)
        gates = [moved_kept] if iteration == 0 else []
        late = [pieces[-1]] if len(pieces) > iteration else []
        if iteration not in LATE:
            gates, late = gates + late, []
        own, sums = call(
            functools.partial(combine_kernel, len(parts)),
            [struct(half_shape, BF16), struct((8, 128))],
            (shifts, state, *parts, *gates),
            [VMEM] * (2 + len(parts)) + [ANY] * len(gates),
        )
        if iteration < ITERS - 1:
            own_other = core_swap(own)
            if iteration:
                late = late + [own_other]
        sums = far_sums(sums, late)
        if iteration < ITERS - 1:
            pair = pack(sec_move(own, 1), sec_move(own, -1))
            if blocks:
                pieces.append(sec_move(blocks[0], 1))
        else:
            pair = pack(sec_move(own, 1), own)
        sums = near_sums(sums)
    pair_other = core_swap(pair)
    final, new_ops = pl.pallas_call(
        functools.partial(finish_kernel, count, tuple(plan)),
        out_shape=(struct(state_start.shape, BF16), struct(left_ops.shape, BF16)),
        in_specs=[VMEM] * (5 + len(pieces)),
        out_specs=(ANY, ANY),
        scratch_shapes=[
            pltpu.VMEM((2 * sectors, width, width), BF16),
            pltpu.VMEM((sectors, width, terms * width), BF16),
            pltpu.VMEM(left_ops.shape, BF16),
            pltpu.SemaphoreType.DMA((units,)),
            pltpu.SemaphoreType.DMA,
        ],
        compiler_params=pltpu.CompilerParams(vmem_limit_bytes=8 * MIB),
        cost_estimate=pl.CostEstimate(
            flops=4 * terms * sectors * width**3, bytes_accessed=4 * MIB, transcendentals=0
        ),
    )(moved_kept, sums, state, pair, pair_other, *pieces)
    return final, new_ops


def solution(mesh):
    in_specs = (
        P("sec", None, None),
        P("op", "sec", None, None),
        P("op", "sec", None, None),
        P("sec"),
        P("op", "sec"),
        P("sec"),
    )
    out_specs = (P("sec", None, None), P("op", "sec", None, None))
    return jax.shard_map(
        per_device, mesh=mesh, in_specs=in_specs, out_specs=out_specs, check_vma=False
    )
```
